256 devices in a mesh: ref: 64 (over z, y_lo, x), win: 4 (over y_hi, core).
Axes of the slice: x: 4, y: 4 (y_hi: 2, y_lo: 2; y = y_hi * 2 + y_lo), z: 8, core: 2. Of those that a mesh axis runs over, the one named last changes fastest.
Arguments:
- queries: bfloat16 [2048, 8192], P('ref', 'win'), may hold values from -1 to 1, as said below
- references: bfloat16 [65536, 8192], P('ref', 'win'), may hold values from -1 to 1, as said below
- labels: int32 [512], P('ref'), may hold values from 0 to 7, as said below
- kernel: float32 [9, 8], replicated, may hold values from 0.02 to 0.3
- class_bias: float32 [8], replicated, may hold values from -4 to 4
Outputs:
- ancestry_logprob: float32 [16, 8, 2048], P('win', None, 'ref')
The draws below stay inside these ranges and needn't reach their ends.
Inputs may be any that keep to these rules, and one draw needn't show every extreme that they name: `queries`: every entry is -1 or +1. `references`: every entry is -1 or +1. Every ancestry labels at least one block.
All inputs are finite; a program needn't handle non-finite values.
Results may differ from the reference program's by a relative error of at most 0.0003.
Values may be sent and summed in bfloat16 or wider, within the bound.
A program may use at most 64 MiB of HBM per device.

```python
import jax
import jax.numpy as jnp
from jax import lax

S = 512
A = 8
BLOCK = 128
TAPS = 9
NQ = 2048
NR = 65536
W = 16
NBLK = 512


def genome_pair(key):
    key_refs = jax.random.fold_in(key, 11)
    key_query = jax.random.fold_in(key, 23)
    key_copy = jax.random.fold_in(key, 37)
    references = (jax.random.randint(key_refs, (NR, W * S), 0, 2) * 2 - 1).astype(jnp.float32)
    queries = (jax.random.randint(key_query, (NQ, W * S), 0, 2) * 2 - 1).astype(jnp.float32)
    copy_count = max(NQ // 8, 1)
    copy_keys = jax.random.split(key_copy, 6)
    copied_rows = jax.random.permutation(copy_keys[0], NQ)[:copy_count]
    source = jax.random.randint(copy_keys[1], (copy_count,), 0, NR // 2) * 2
    twin_rows = source + 1
    window_sites = jnp.arange(S)
    first_site = jax.random.randint(copy_keys[2], (copy_count, W, 1), 0, S)
    flip_mask = (window_sites == first_site).reshape(copy_count, W * S)
    source_rows = references[source]
    references = references.at[twin_rows].set(jnp.where(flip_mask, -source_rows, source_rows))
    levels = jnp.array([0, S // 32, S // 16], dtype=jnp.int32)
    strength = levels[jax.random.randint(copy_keys[4], (copy_count,), 0, 3)]
    noise_mask = jax.random.randint(copy_keys[5], (copy_count, W * S), 0, S) < strength[:, None]
    queries = queries.at[copied_rows].set(jnp.where(noise_mask, -source_rows, source_rows))
    return (references, queries)


def draw_queries(key, part):
    return genome_pair(key)[1].astype(jnp.bfloat16)


def draw_references(key, part):
    return genome_pair(key)[0].astype(jnp.bfloat16)


def draw_labels(key, part):
    key_label = jax.random.fold_in(key, 51)
    key_place = jax.random.fold_in(key, 53)
    labels = jax.random.randint(key_label, (NBLK,), 0, A)
    placed = jax.random.permutation(key_place, NBLK)[:A]
    return labels.at[placed].set(jnp.arange(A, dtype=jnp.int32)).astype(jnp.int32)


def noise(stream_key, extent, deviation, most, kind=jnp.bfloat16):
    values = jax.random.normal(stream_key, extent, jnp.float32) * deviation
    return jnp.minimum(jnp.maximum(values, -most), most).astype(kind)


def setup_inputs(seed: int = 0) -> dict:
    seeds = jax.random.split(jax.random.key(seed), 6)
    return {
        "queries": draw_queries(jax.random.fold_in(seeds[5], 71), 0),
        "references": draw_references(jax.random.fold_in(seeds[5], 71), 0),
        "labels": draw_labels(jax.random.fold_in(seeds[5], 71), 0),
        "kernel": jnp.clip(jax.random.uniform(seeds[3], (TAPS, A), jnp.float32, 0.02, 0.3), 0.02, 0.3),
        "class_bias": noise(seeds[4], (A,), 1.0, 4.0, jnp.float32),
    }


def reference(queries, references, labels, kernel, class_bias):
    owner_label = jnp.repeat(labels, BLOCK)
    score_scale = 256.0 / S

    def pooled_window(window):
        start_col = (window * S).astype(jnp.int32)
        query_part = lax.dynamic_slice_in_dim(queries, start_col, S, 1)
        ref_part = lax.dynamic_slice_in_dim(references, start_col, S, 1)
        scores = jnp.dot(query_part, ref_part.T, preferred_element_type=jnp.float32) * score_scale

        def ancestry_lse(ancestry):
            member = (owner_label == ancestry).astype(scores.dtype)
            return jax.nn.logsumexp(scores, axis=1, b=member[None, :])

        return lax.map(ancestry_lse, jnp.arange(A, dtype=jnp.int32))

    pooled = lax.map(pooled_window, jnp.arange(W, dtype=jnp.int32))
    centered = pooled - jnp.mean(pooled, axis=1, keepdims=True)
    half_width = TAPS // 2
    padded = jnp.pad(centered, ((half_width, half_width), (0, 0), (0, 0)))
    smoothed = jnp.zeros_like(centered)
    for offset in range(TAPS):
        smoothed = smoothed + kernel[offset][None, :, None] * padded[offset:offset + W]
    logits = smoothed + class_bias[None, :, None]
    return jax.nn.log_softmax(logits, axis=1)
```

```python
import functools

import jax
import jax.numpy as jnp
from jax import lax
from jax.experimental import pallas as pl
from jax.experimental.pallas import tpu as pltpu
from jax.sharding import PartitionSpec as P

S = 512
A = 8
BLOCK = 128
TAPS = 9
NX, NY, NZ = 4, 2, 8
ROWS = 32
WIN = 4
REFS = 1024
NB = REFS // BLOCK
PLANE = NX * NY
LANES = WIN * ROWS
FLOOR = -1e30
MESH = pl.DeviceIdType.MESH


class Ids:
    def __init__(self):
        self.numbers = {}

    def __call__(self, *name):
        return self.numbers.setdefault(name, len(self.numbers))


def lse(values):
    peak = functools.reduce(jnp.maximum, values)
    total = functools.reduce(jnp.add, [jnp.exp(v - peak) for v in values])
    return peak + jnp.log(total)


def body(ids, q_ref, r_ref, lab_ref, ker_ref, bias_ref, out_ref,
         g, refs, pen, part, sbuf, r1, zbuf, r2, cent, halo, ssem, rsem, lsem):
    ref = lax.axis_index("ref")
    win = lax.axis_index("win")
    z, y, x = ref // PLANE, (ref // NX) % NY, ref % NX
    ny = 1 - y

    def at(zz, yy, xx):
        return {"ref": zz * PLANE + yy * NX + xx}

    def zz(delta):
        return (z + delta + NZ) % NZ

    def xx(delta):
        return (x + delta + NX) % NX

    local = []
    for w in range(WIN):
        local.append(pltpu.make_async_copy(
            q_ref.at[:, pl.ds(w * S, S)], g.at[w, z, y, x], lsem.at[w]))
    for w in range(WIN):
        local.append(pltpu.make_async_copy(
            r_ref.at[:, pl.ds(w * S, S)], refs.at[w], lsem.at[WIN + w]))
    for copy in local:
        copy.start()

    barrier = pltpu.get_barrier_semaphore()
    peers = [at(z, (y + dy) % NY, xx(dx)) for dy in range(NY) for dx in range(NX) if dy or dx]
    peers += [at(zz(d), y, x) for d in range(1, NZ)]
    peers += [{"win": (win + 1) % WIN}, {"win": (win + WIN - 1) % WIN}]
    for peer in peers:
        pl.semaphore_signal(barrier, inc=1, device_id=peer, device_id_type=MESH)

    ancestry = lax.broadcasted_iota(jnp.int32, (A, 2 * LANES), 0)
    for b in range(NB):
        pen[b] = jnp.where(ancestry == lab_ref[b], 0.0, FLOOR)

    pl.semaphore_wait(barrier, len(peers))
    for copy in local[:WIN]:
        copy.wait()

    sent = []

    def copy_of(name, src, dst, device):
        n = ids(*name)
        return pltpu.make_async_remote_copy(
            src_ref=src, dst_ref=dst, send_sem=ssem.at[n], recv_sem=rsem.at[n],
            device_id=device, device_id_type=MESH)

    def send(name, src, device, dst=None):
        copy = copy_of(name, src, src if dst is None else dst, device)
        copy.start()
        sent.append(copy)

    def recv(name, dst):
        copy_of(name, dst, dst, at(z, ny, x)).wait_recv()

    right, left = at(z, y, xx(1)), at(z, y, xx(-1))
    other = at(z, ny, x)
    down = {1: at(zz(-1), y, x), -1: at(zz(1), y, x)}
    signs = (1, -1)
    two = pl.ds(0, 2)
    ad, bb = pl.ds(0, 2), pl.ds(2, 2)
    both = pl.ds(0, NY)

    own = g.at[pl.ds(0, WIN), z, y, x]
    send(("x0", 0), g.at[ad, z, y, x], right)
    send(("x0", 1), g.at[ad, z, y, x], left)
    send(("y0", 0), own, other)
    for s in signs:
        send(("z1", s, 0), own, down[s])

    def x_stage(zb):
        def start():
            send(("bx", zb, 0), g.at[bb, zz(zb), both, x], right)
            send(("bx", zb, 1), g.at[bb, zz(zb), both, x], left)

        def forward():
            recv(("bx", zb, 0), g.at[bb, zz(zb), both, xx(-1)])
            send(("bf", zb, 0), g.at[2, zz(zb), both, xx(-1)], right)
            recv(("bx", zb, 1), g.at[bb, zz(zb), both, xx(1)])
            send(("bf", zb, 1), g.at[3, zz(zb), both, xx(1)], left)

        def finish():
            recv(("bf", zb, 0), g.at[2, zz(zb), both, xx(2)])
            recv(("bf", zb, 1), g.at[3, zz(zb), both, xx(2)])

        return start, forward, finish

    def y_start(zb):
        send(("dy", zb), g.at[1, zz(zb), y], other)

    def y_finish(zb):
        recv(("dy", zb), g.at[1, zz(zb), ny])

    stages = {zb: x_stage(zb) for zb in (0, 1, -1, 2, -2, 3, -3, 4)}

    recv(("y0", 0), g.at[pl.ds(0, WIN), z, ny, x])
    for s in signs:
        send(("z1", s, 1), g.at[bb, z, ny, x], down[s])
    recv(("x0", 0), g.at[ad, z, y, xx(-1)])
    send(("xf", 0), g.at[0, z, y, xx(-1)], right)
    recv(("x0", 1), g.at[ad, z, y, xx(1)])
    send(("xf", 1), g.at[1, z, y, xx(1)], left)
    stages[0][0]()
    for n, dx in ((1, -1), (2, 1)):
        send(("y0", n), g.at[ad, z, y, xx(dx)], other)
        for s in signs:
            send(("z1", s, 1 + n), g.at[ad, z, y, xx(dx)], down[s])
    recv(("xf", 0), g.at[0, z, y, xx(2)])
    recv(("xf", 1), g.at[1, z, y, xx(2)])
    send(("y0", 3), g.at[ad, z, y, xx(2)], other)
    for s in signs:
        send(("z1", s, 4), g.at[ad, z, y, xx(2)], down[s])
    for n, dx in ((1, -1), (2, 1), (3, 2)):
        recv(("y0", n), g.at[ad, z, ny, xx(dx)])
    for s in signs:
        send(("z1", s, 5), g.at[0, z, ny], down[s])

    def b_part(k, s):
        zb = zz(s * k)
        if k < 4:
            return g.at[bb, zb, both, x]
        return g.at[2 if s == 1 else 3, zb, both, x]

    def d_part(k, s):
        zb = zz(s * k)
        if k < 4:
            return g.at[1, zb, y]
        return g.at[1, zb, y, pl.ds(0 if s == 1 else 2, 2)]

    def a_part(k, s):
        zb = zz(s * k)
        if k < 4:
            return g.at[0, zb]
        return g.at[0, zb, 0 if s == 1 else 1]

    parts = {"b": b_part, "d": d_part, "a": a_part}

    def pass_on(kind, k, s):
        zb = zz(s * (k - 1))
        if kind == "b":
            src = g.at[bb, zb, both, x] if k < 4 else g.at[2 if s == 1 else 3, zb, both, x]
        elif kind == "d":
            src = g.at[1, zb, y] if k < 4 else g.at[1, zb, y, pl.ds(0 if s == 1 else 2, 2)]
        else:
            src = g.at[0, zb] if k < 4 else g.at[0, zb, 0 if s == 1 else 1]
        send((kind, k, s), src, down[s])

    def take(kind, k, s):
        recv((kind, k, s), parts[kind](k, s))

    def score(w, zb, slot):
        queries = g[w, zb].reshape(2 * LANES, S)
        peaks, totals = [], []
        for b in range(NB):
            scores = lax.dot_general(
                refs[w, b * BLOCK:(b + 1) * BLOCK, :], queries, (((1,), (1,)), ((), ())),
                preferred_element_type=jnp.float32)
            peak = jnp.max(scores, axis=0, keepdims=True)
            totals.append(jnp.sum(jnp.exp((scores - peak) * (256.0 / S)), axis=0, keepdims=True))
            peaks.append(peak * (256.0 / S))
        shifted = [peaks[b] + pen[b] for b in range(NB)]
        top = functools.reduce(jnp.maximum, shifted)
        total = functools.reduce(
            jnp.add, [totals[b] * jnp.exp(shifted[b] - top) for b in range(NB)])
        part[slot, w] = top + jnp.log(total)

    def blocks_of(k):
        return (0,) if k == 0 else (4,) if k == 4 else (k, -k)

    def compute(k, w_from, w_to):
        n = w_to - w_from
        count = len(blocks_of(k))

        def one(i, carry):
            slot, w = i // n, w_from + i % n
            zb = zz(k * (1 - 2 * slot))
            score(w, zb, slot)
            return carry

        lax.fori_loop(0, n * count, one, 0)

    lane = lax.broadcasted_iota(jnp.int32, (A, LANES), 1) // ROWS

    def plane_send(k):
        count = len(blocks_of(k))
        for slot in range(count):
            for o in range(PLANE):
                half = pl.ds((o // WIN) * LANES, LANES)
                packed = None
                for w in range(WIN):
                    shift = ((w - o) % WIN) * ROWS
                    piece = part[slot, w, :, half]
                    piece = pltpu.roll(piece, shift, 1) if shift else piece
                    packed = piece if packed is None else jnp.where(lane == w, piece, packed)
                sbuf[k, o, slot] = packed
        span = pl.ds(0, count)
        for dy in range(NY):
            for dx in range(NX):
                if dy or dx:
                    ty, tx = (y + dy) % NY, xx(dx)
                    send(("p", k, dy, dx), sbuf.at[k, ty * NX + tx, span], at(z, ty, tx),
                         r1.at[k, dy * NX + dx, span])

    def plane_combine(k):
        count = len(blocks_of(k))
        span = pl.ds(0, count)
        for dy in range(NY):
            for dx in range(NX):
                if dy or dx:
                    recv(("p", k, dy, dx), r1.at[k, dy * NX + dx, span])
        for slot, zb in enumerate(blocks_of(k)):
            mine = lse([sbuf[k, y * NX + x, slot]] + [r1[k, n, slot] for n in range(1, PLANE)])
            n = zb % NZ
            zbuf[n] = mine
            if zb:
                send(("r", n), zbuf.at[n], at(zz(zb), y, x), r2.at[n])

    for s in signs:
        recv(("z1", s, 0), g.at[pl.ds(0, WIN), zz(s), y, x])
        recv(("z1", s, 1), g.at[bb, zz(s), ny, x])
        pass_on("b", 2, s)
        stages[s][0]()
    for s in signs:
        for n, dx in ((2, -1), (3, 1), (4, 2)):
            recv(("z1", s, n), g.at[ad, zz(s), y, xx(dx)])
        pass_on("d", 2, s)
        y_start(s)
    for copy in local[WIN:]:
        copy.wait()
    stages[0][1]()
    compute(0, 0, 2)
    for s in signs:
        recv(("z1", s, 5), g.at[0, zz(s), ny])
        pass_on("a", 2, s)
    stages[0][2]()
    compute(0, 2, 4)
    plane_send(0)
    for s in signs:
        stages[s][1]()

    for k in (2, 3):
        for s in signs:
            take("b", k, s)
            pass_on("b", k + 1, s)
            stages[s * k][0]()
        for s in signs:
            take("d", k, s)
            pass_on("d", k + 1, s)
            y_start(s * k)
        for s in signs:
            y_finish(s * (k - 1))
            stages[s * (k - 1)][2]()
        compute(k - 1, 0, 4)
        plane_send(k - 1)
        for s in signs:
            take("a", k, s)
            pass_on("a", k + 1, s)
        for s in signs:
            stages[s * k][1]()
        plane_combine(k - 2)

    for s in signs:
        take("b", 4, s)
    stages[4][0]()
    for s in signs:
        take("d", 4, s)
    y_start(4)
    for s in signs:
        y_finish(s * 3)
        stages[s * 3][2]()
    compute(3, 0, 4)
    plane_send(3)
    stages[4][1]()
    plane_combine(2)
    for s in signs:
        take("a", 4, s)
    y_finish(4)
    compute(4, 0, 2)
    stages[4][2]()
    compute(4, 2, 4)
    plane_send(4)
    plane_combine(3)
    plane_combine(4)

    for n in range(1, NZ):
        recv(("r", n), r2.at[n])
    pooled = lse([zbuf[0]] + [r2[n] for n in range(1, NZ)])
    centered = pooled - jnp.mean(pooled, axis=0, keepdims=True)
    cent[...] = centered
    send(("h", 0), cent, {"win": (win + 1) % WIN}, halo.at[0])
    send(("h", 1), cent, {"win": (win + WIN - 1) % WIN}, halo.at[1])

    def column(read):
        rows = lax.broadcasted_iota(jnp.int32, (A, LANES), 0)
        value = jnp.full((A, LANES), read(0), jnp.float32)
        for a in range(1, A):
            value = jnp.where(rows == a, read(a), value)
        return value

    taps = [column(lambda a, t=t: ker_ref[t, a]) for t in range(TAPS)]
    bias = column(lambda a: bias_ref[a])
    recv(("h", 0), halo.at[0])
    recv(("h", 1), halo.at[1])
    low = jnp.where(win > 0, halo[0], 0.0)
    high = jnp.where(win < WIN - 1, halo[1], 0.0)
    logits = bias
    for t in range(TAPS):
        d = t - TAPS // 2
        if d == 0:
            moved = centered
        elif d < 0:
            shift = (-d * ROWS) % LANES
            moved = low if not shift else jnp.where(
                lane < -d, pltpu.roll(low, shift, 1), pltpu.roll(centered, shift, 1))
        else:
            shift = (-d * ROWS) % LANES
            moved = high if not shift else jnp.where(
                lane >= WIN - d, pltpu.roll(high, shift, 1), pltpu.roll(centered, shift, 1))
        logits = logits + taps[t] * moved
    peak = jnp.max(logits, axis=0, keepdims=True)
    result = logits - peak - jnp.log(jnp.sum(jnp.exp(logits - peak), axis=0, keepdims=True))
    for w in range(WIN):
        out_ref[w] = result[:, w * ROWS:(w + 1) * ROWS]

    for copy in sent:
        copy.wait_send()


MESSAGES = 160


def per_device(queries, references, labels, kernel, class_bias):
    ids = Ids()
    hbm = pl.BlockSpec(memory_space=pl.ANY)
    smem = pl.BlockSpec(memory_space=pltpu.SMEM)
    return pl.pallas_call(
        functools.partial(body, ids),
        out_shape=jax.ShapeDtypeStruct((WIN, A, ROWS), jnp.float32),
        in_specs=[hbm, hbm, smem, smem, smem],
        out_specs=pl.BlockSpec(memory_space=pltpu.VMEM),
        scratch_shapes=[
            pltpu.VMEM((WIN, NZ, NY, NX, ROWS, S), jnp.bfloat16),
            pltpu.VMEM((WIN, REFS, S), jnp.bfloat16),
            pltpu.VMEM((NB, A, 2 * LANES), jnp.float32),
            pltpu.VMEM((2, WIN, A, 2 * LANES), jnp.float32),
            pltpu.VMEM((5, PLANE, 2, A, LANES), jnp.float32),
            pltpu.VMEM((5, PLANE, 2, A, LANES), jnp.float32),
            pltpu.VMEM((NZ, A, LANES), jnp.float32),
            pltpu.VMEM((NZ, A, LANES), jnp.float32),
            pltpu.VMEM((A, LANES), jnp.float32),
            pltpu.VMEM((2, A, LANES), jnp.float32),
            pltpu.SemaphoreType.DMA((MESSAGES,)),
            pltpu.SemaphoreType.DMA((MESSAGES,)),
            pltpu.SemaphoreType.DMA((2 * WIN,)),
        ],
        compiler_params=pltpu.CompilerParams(
            collective_id=0, has_side_effects=True, vmem_limit_bytes=48 * 1024 * 1024),
        cost_estimate=pl.CostEstimate(
            flops=2 * 2048 * REFS * S * WIN, bytes_accessed=5 * 1024 * 1024,
            transcendentals=2048 * REFS * WIN),
    )(queries, references, labels, kernel, class_bias)


def solution(mesh):
    in_specs = (P("ref", "win"), P("ref", "win"), P("ref"), P(), P())
    out_specs = P("win", None, "ref")
    return jax.shard_map(
        per_device, mesh=mesh, in_specs=in_specs, out_specs=out_specs, check_vma=False
    )
```

```python
import functools

import jax
import jax.numpy as jnp
from jax import lax
from jax.experimental import pallas as pl
from jax.experimental.pallas import tpu as pltpu
from jax.sharding import PartitionSpec as P

S = 512
A = 8
BLOCK = 128
TAPS = 9
NX, NY, NZ = 4, 2, 8
ROWS = 32
WIN = 4
REFS = 1024
NB = REFS // BLOCK
PLANE = NX * NY
LANES = WIN * ROWS
FLOOR = -1e30
SCALE = 256.0 / S
SCALE_2 = SCALE * 1.4426950408889634
MESH = pl.DeviceIdType.MESH


class Ids:
    def __init__(self):
        self.numbers = {}

    def __call__(self, *name):
        return self.numbers.setdefault(name, len(self.numbers))


def lse(values):
    peak = functools.reduce(jnp.maximum, values)
    total = functools.reduce(jnp.add, [jnp.exp(v - peak) for v in values])
    return peak + jnp.log(total)


def body(ids, q_ref, r_ref, lab_ref, ker_ref, bias_ref, out_ref,
         g, refs, pen, part, sbuf, r1, zbuf, r2, cent, halo, ssem, rsem, lsem):
    ref = lax.axis_index("ref")
    win = lax.axis_index("win")
    z, y, x = ref // PLANE, (ref // NX) % NY, ref % NX
    ny = 1 - y

    def at(zz, yy, xx):
        return {"ref": zz * PLANE + yy * NX + xx}

    def zz(delta):
        return (z + delta + NZ) % NZ

    def xx(delta):
        return (x + delta + NX) % NX

    local = []
    for w in range(WIN):
        local.append(pltpu.make_async_copy(
            q_ref.at[:, pl.ds(w * S, S)], g.at[w, z, y, x], lsem.at[w]))
    for w in range(WIN):
        local.append(pltpu.make_async_copy(
            r_ref.at[:, pl.ds(w * S, S)], refs.at[w], lsem.at[WIN + w]))
    for copy in local:
        copy.start()

    barrier = pltpu.get_barrier_semaphore()
    peers = [at(z, (y + dy) % NY, xx(dx)) for dy in range(NY) for dx in range(NX) if dy or dx]
    peers += [at(zz(d), y, x) for d in range(1, NZ)]
    peers += [{"win": (win + 1) % WIN}, {"win": (win + WIN - 1) % WIN}]
    for peer in peers:
        pl.semaphore_signal(barrier, inc=1, device_id=peer, device_id_type=MESH)

    ancestry = lax.broadcasted_iota(jnp.int32, (A, 2 * LANES), 0)
    for b in range(NB):
        pen[b] = jnp.where(ancestry == lab_ref[b], 0.0, FLOOR)

    pl.semaphore_wait(barrier, len(peers))
    for copy in local[:WIN]:
        copy.wait()

    sent = []

    def copy_of(name, src, dst, device):
        n = ids(*name)
        return pltpu.make_async_remote_copy(
            src_ref=src, dst_ref=dst, send_sem=ssem.at[n], recv_sem=rsem.at[n],
            device_id=device, device_id_type=MESH)

    def send(name, src, device, dst=None):
        copy = copy_of(name, src, src if dst is None else dst, device)
        copy.start()
        sent.append(copy)

    def recv(name, dst):
        copy_of(name, dst, dst, at(z, ny, x)).wait_recv()

    right, left = at(z, y, xx(1)), at(z, y, xx(-1))
    other = at(z, ny, x)
    down = {1: at(zz(-1), y, x), -1: at(zz(1), y, x)}
    signs = (1, -1)
    two = pl.ds(0, 2)
    ad, bb = pl.ds(0, 2), pl.ds(2, 2)
    both = pl.ds(0, NY)

    own = g.at[pl.ds(0, WIN), z, y, x]
    send(("x0", 0), g.at[ad, z, y, x], right)
    send(("x0", 1), g.at[ad, z, y, x], left)
    send(("y0", 0), own, other)
    for s in signs:
        send(("z1", s, 0), own, down[s])

    def x_stage(zb):
        def start():
            send(("bx", zb, 0), g.at[bb, zz(zb), both, x], right)
            send(("bx", zb, 1), g.at[bb, zz(zb), both, x], left)

        def forward():
            recv(("bx", zb, 0), g.at[bb, zz(zb), both, xx(-1)])
            send(("bf", zb, 0), g.at[2, zz(zb), both, xx(-1)], right)
            recv(("bx", zb, 1), g.at[bb, zz(zb), both, xx(1)])
            send(("bf", zb, 1), g.at[3, zz(zb), both, xx(1)], left)

        def finish():
            recv(("bf", zb, 0), g.at[2, zz(zb), both, xx(2)])
            recv(("bf", zb, 1), g.at[3, zz(zb), both, xx(2)])

        return start, forward, finish

    def y_start(zb):
        send(("dy", zb), g.at[1, zz(zb), y], other)

    def y_finish(zb):
        recv(("dy", zb), g.at[1, zz(zb), ny])

    stages = {zb: x_stage(zb) for zb in (0, 1, -1, 2, -2, 3, -3, 4)}

    recv(("y0", 0), g.at[pl.ds(0, WIN), z, ny, x])
    for s in signs:
        send(("z1", s, 1), g.at[bb, z, ny, x], down[s])
    recv(("x0", 0), g.at[ad, z, y, xx(-1)])
    send(("xf", 0), g.at[0, z, y, xx(-1)], right)
    recv(("x0", 1), g.at[ad, z, y, xx(1)])
    send(("xf", 1), g.at[1, z, y, xx(1)], left)
    stages[0][0]()
    for n, dx in ((1, -1), (2, 1)):
        send(("y0", n), g.at[ad, z, y, xx(dx)], other)
        for s in signs:
            send(("z1", s, 1 + n), g.at[ad, z, y, xx(dx)], down[s])
    recv(("xf", 0), g.at[0, z, y, xx(2)])
    recv(("xf", 1), g.at[1, z, y, xx(2)])
    send(("y0", 3), g.at[ad, z, y, xx(2)], other)
    for s in signs:
        send(("z1", s, 4), g.at[ad, z, y, xx(2)], down[s])
    for n, dx in ((1, -1), (2, 1), (3, 2)):
        recv(("y0", n), g.at[ad, z, ny, xx(dx)])
    for s in signs:
        send(("z1", s, 5), g.at[0, z, ny], down[s])

    def b_part(k, s):
        zb = zz(s * k)
        if k < 4:
            return g.at[bb, zb, both, x]
        return g.at[2 if s == 1 else 3, zb, both, x]

    def d_part(k, s):
        zb = zz(s * k)
        if k < 4:
            return g.at[1, zb, y]
        return g.at[1, zb, y, pl.ds(0 if s == 1 else 2, 2)]

    def a_part(k, s):
        zb = zz(s * k)
        if k < 4:
            return g.at[0, zb]
        return g.at[0, zb, 0 if s == 1 else 1]

    parts = {"b": b_part, "d": d_part, "a": a_part}

    def pass_on(kind, k, s):
        zb = zz(s * (k - 1))
        if kind == "b":
            src = g.at[bb, zb, both, x] if k < 4 else g.at[2 if s == 1 else 3, zb, both, x]
        elif kind == "d":
            src = g.at[1, zb, y] if k < 4 else g.at[1, zb, y, pl.ds(0 if s == 1 else 2, 2)]
        else:
            src = g.at[0, zb] if k < 4 else g.at[0, zb, 0 if s == 1 else 1]
        send((kind, k, s), src, down[s])

    def take(kind, k, s):
        recv((kind, k, s), parts[kind](k, s))

    def score(w, zb, slot):
        queries = g[w, zb].reshape(2 * LANES, S)
        group = lax.dot_general(
            refs[w], queries, (((1,), (1,)), ((), ())), preferred_element_type=jnp.float32)
        peaks, totals = [], []
        for b in range(NB):
            scores = group[b * BLOCK:(b + 1) * BLOCK]
            peak = jnp.max(scores, axis=0, keepdims=True)
            totals.append(jnp.sum(jnp.exp2((scores - peak) * SCALE_2), axis=0, keepdims=True))
            peaks.append(peak * SCALE)
        shifted = [peaks[b] + pen[b] for b in range(NB)]
        top = functools.reduce(jnp.maximum, shifted)
        total = functools.reduce(
            jnp.add, [totals[b] * jnp.exp(shifted[b] - top) for b in range(NB)])
        part[slot, w] = top + jnp.log(total)

    def blocks_of(k):
        return (0,) if k == 0 else (4,) if k == 4 else (k, -k)

    def compute(k, w_from, w_to):
        n = w_to - w_from
        count = len(blocks_of(k))

        def one(i, carry):
            slot, w = i // n, w_from + i % n
            zb = zz(k * (1 - 2 * slot))
            score(w, zb, slot)
            return carry

        lax.fori_loop(0, n * count, one, 0)

    lane = lax.broadcasted_iota(jnp.int32, (A, LANES), 1) // ROWS

    def plane_send(k):
        count = len(blocks_of(k))
        for slot in range(count):
            for o in range(PLANE):
                half = pl.ds((o // WIN) * LANES, LANES)
                packed = None
                for w in range(WIN):
                    shift = ((w - o) % WIN) * ROWS
                    piece = part[slot, w, :, half]
                    piece = pltpu.roll(piece, shift, 1) if shift else piece
                    packed = piece if packed is None else jnp.where(lane == w, piece, packed)
                sbuf[k, o, slot] = packed
        span = pl.ds(0, count)
        for dy in range(NY):
            for dx in range(NX):
                if dy or dx:
                    ty, tx = (y + dy) % NY, xx(dx)
                    send(("p", k, dy, dx), sbuf.at[k, ty * NX + tx, span], at(z, ty, tx),
                         r1.at[k, dy * NX + dx, span])

    def plane_combine(k):
        count = len(blocks_of(k))
        span = pl.ds(0, count)
        for dy in range(NY):
            for dx in range(NX):
                if dy or dx:
                    recv(("p", k, dy, dx), r1.at[k, dy * NX + dx, span])
        for slot, zb in enumerate(blocks_of(k)):
            mine = lse([sbuf[k, y * NX + x, slot]] + [r1[k, n, slot] for n in range(1, PLANE)])
            n = zb % NZ
            zbuf[n] = mine
            if zb:
                send(("r", n), zbuf.at[n], at(zz(zb), y, x), r2.at[n])

    for s in signs:
        recv(("z1", s, 0), g.at[pl.ds(0, WIN), zz(s), y, x])
        recv(("z1", s, 1), g.at[bb, zz(s), ny, x])
        pass_on("b", 2, s)
        stages[s][0]()
    for s in signs:
        for n, dx in ((2, -1), (3, 1), (4, 2)):
            recv(("z1", s, n), g.at[ad, zz(s), y, xx(dx)])
        pass_on("d", 2, s)
        y_start(s)
    for copy in local[WIN:]:
        copy.wait()
    stages[0][1]()
    compute(0, 0, 2)
    for s in signs:
        recv(("z1", s, 5), g.at[0, zz(s), ny])
        pass_on("a", 2, s)
    stages[0][2]()
    compute(0, 2, 4)
    plane_send(0)
    for s in signs:
        stages[s][1]()

    for k in (2, 3):
        for s in signs:
            take("b", k, s)
            pass_on("b", k + 1, s)
            stages[s * k][0]()
        for s in signs:
            take("d", k, s)
            pass_on("d", k + 1, s)
            y_start(s * k)
        for s in signs:
            y_finish(s * (k - 1))
            stages[s * (k - 1)][2]()
        compute(k - 1, 0, 4)
        plane_send(k - 1)
        for s in signs:
            take("a", k, s)
            pass_on("a", k + 1, s)
        for s in signs:
            stages[s * k][1]()
        plane_combine(k - 2)

    for s in signs:
        take("b", 4, s)
    stages[4][0]()
    for s in signs:
        take("d", 4, s)
    y_start(4)
    for s in signs:
        y_finish(s * 3)
        stages[s * 3][2]()
    compute(3, 0, 4)
    plane_send(3)
    stages[4][1]()
    plane_combine(2)
    for s in signs:
        take("a", 4, s)
    y_finish(4)
    compute(4, 0, 2)
    stages[4][2]()
    compute(4, 2, 4)
    plane_send(4)
    plane_combine(3)
    plane_combine(4)

    for n in range(1, NZ):
        recv(("r", n), r2.at[n])
    pooled = lse([zbuf[0]] + [r2[n] for n in range(1, NZ)])
    centered = pooled - jnp.mean(pooled, axis=0, keepdims=True)
    cent[...] = centered
    send(("h", 0), cent, {"win": (win + 1) % WIN}, halo.at[0])
    send(("h", 1), cent, {"win": (win + WIN - 1) % WIN}, halo.at[1])

    def column(read):
        rows = lax.broadcasted_iota(jnp.int32, (A, LANES), 0)
        value = jnp.full((A, LANES), read(0), jnp.float32)
        for a in range(1, A):
            value = jnp.where(rows == a, read(a), value)
        return value

    taps = [column(lambda a, t=t: ker_ref[a, t]) for t in range(TAPS)]
    bias = column(lambda a: bias_ref[a])
    recv(("h", 0), halo.at[0])
    recv(("h", 1), halo.at[1])
    low = jnp.where(win > 0, halo[0], 0.0)
    high = jnp.where(win < WIN - 1, halo[1], 0.0)
    logits = bias
    for t in range(TAPS):
        d = t - TAPS // 2
        if d == 0:
            moved = centered
        elif d < 0:
            shift = (-d * ROWS) % LANES
            moved = low if not shift else jnp.where(
                lane < -d, pltpu.roll(low, shift, 1), pltpu.roll(centered, shift, 1))
        else:
            shift = (-d * ROWS) % LANES
            moved = high if not shift else jnp.where(
                lane >= WIN - d, pltpu.roll(high, shift, 1), pltpu.roll(centered, shift, 1))
        logits = logits + taps[t] * moved
    peak = jnp.max(logits, axis=0, keepdims=True)
    result = logits - peak - jnp.log(jnp.sum(jnp.exp(logits - peak), axis=0, keepdims=True))
    for w in range(WIN):
        out_ref[w] = result[:, w * ROWS:(w + 1) * ROWS]

    for copy in sent:
        copy.wait_send()


MESSAGES = 160


def per_device(queries, references, labels, kernel, class_bias):
    ids = Ids()
    hbm = pl.BlockSpec(memory_space=pl.ANY)
    smem = pl.BlockSpec(memory_space=pltpu.SMEM)
    return pl.pallas_call(
        functools.partial(body, ids),
        out_shape=jax.ShapeDtypeStruct((WIN, A, ROWS), jnp.float32),
        in_specs=[hbm, hbm, smem, smem, smem],
        out_specs=pl.BlockSpec(memory_space=pltpu.VMEM),
        scratch_shapes=[
            pltpu.VMEM((WIN, NZ, NY, NX, ROWS, S), jnp.bfloat16),
            pltpu.VMEM((WIN, REFS, S), jnp.bfloat16),
            pltpu.VMEM((NB, A, 2 * LANES), jnp.float32),
            pltpu.VMEM((2, WIN, A, 2 * LANES), jnp.float32),
            pltpu.VMEM((5, PLANE, 2, A, LANES), jnp.float32),
            pltpu.VMEM((5, PLANE, 2, A, LANES), jnp.float32),
            pltpu.VMEM((NZ, A, LANES), jnp.float32),
            pltpu.VMEM((NZ, A, LANES), jnp.float32),
            pltpu.VMEM((A, LANES), jnp.float32),
            pltpu.VMEM((2, A, LANES), jnp.float32),
            pltpu.SemaphoreType.DMA((MESSAGES,)),
            pltpu.SemaphoreType.DMA((MESSAGES,)),
            pltpu.SemaphoreType.DMA((2 * WIN,)),
        ],
        compiler_params=pltpu.CompilerParams(
            collective_id=0, has_side_effects=True, vmem_limit_bytes=60 * 1024 * 1024),
        cost_estimate=pl.CostEstimate(
            flops=2 * 2048 * REFS * S * WIN, bytes_accessed=5 * 1024 * 1024,
            transcendentals=2048 * REFS * WIN),
    )(queries, references, labels, kernel.T, class_bias)


def solution(mesh):
    in_specs = (P("ref", "win"), P("ref", "win"), P("ref"), P(), P())
    out_specs = P("win", None, "ref")
    return jax.shard_map(
        per_device, mesh=mesh, in_specs=in_specs, out_specs=out_specs, check_vma=False
    )
```

```python
import functools

import jax
import jax.numpy as jnp
from jax import lax
from jax.experimental import pallas as pl
from jax.experimental.pallas import tpu as pltpu
from jax.sharding import PartitionSpec as P

S = 512
A = 8
BLOCK = 128
TAPS = 9
NX, NY, NZ = 4, 2, 8
ROWS = 32
WIN = 4
REFS = 1024
NB = REFS // BLOCK
PLANE = NX * NY
LANES = WIN * ROWS
FLOOR = -1e30
EXACT = jnp.float8_e4m3fn
SCALE = 256.0 / S
SCALE_2 = SCALE * 1.4426950408889634
MESH = pl.DeviceIdType.MESH


class Ids:
    def __init__(self):
        self.numbers = {}

    def __call__(self, *name):
        return self.numbers.setdefault(name, len(self.numbers))


def lse(values):
    peak = functools.reduce(jnp.maximum, values)
    total = functools.reduce(jnp.add, [jnp.exp(v - peak) for v in values])
    return peak + jnp.log(total)


def body(ids, q_ref, r_ref, lab_ref, ker_ref, bias_ref, out_ref,
         g, refs, pen, part, sbuf, r1, zbuf, r2, cent, halo, refs8, ssem, rsem, lsem):
    ref = lax.axis_index("ref")
    win = lax.axis_index("win")
    z, y, x = ref // PLANE, (ref // NX) % NY, ref % NX
    ny = 1 - y

    def at(zz, yy, xx):
        return {"ref": zz * PLANE + yy * NX + xx}

    def zz(delta):
        return (z + delta + NZ) % NZ

    def xx(delta):
        return (x + delta + NX) % NX

    local = []
    for w in range(WIN):
        local.append(pltpu.make_async_copy(
            q_ref.at[:, pl.ds(w * S, S)], g.at[w, z, y, x], lsem.at[w]))
    for w in range(WIN):
        local.append(pltpu.make_async_copy(
            r_ref.at[:, pl.ds(w * S, S)], refs.at[w], lsem.at[WIN + w]))
    for copy in local:
        copy.start()

    barrier = pltpu.get_barrier_semaphore()
    peers = [at(z, (y + dy) % NY, xx(dx)) for dy in range(NY) for dx in range(NX) if dy or dx]
    peers += [at(zz(d), y, x) for d in range(1, NZ)]
    peers += [{"win": (win + 1) % WIN}, {"win": (win + WIN - 1) % WIN}]
    for peer in peers:
        pl.semaphore_signal(barrier, inc=1, device_id=peer, device_id_type=MESH)

    ancestry = lax.broadcasted_iota(jnp.int32, (A, 2 * LANES), 0)
    for b in range(NB):
        pen[b] = jnp.where(ancestry == lab_ref[b], 0.0, FLOOR)

    pl.semaphore_wait(barrier, len(peers))
    for copy in local[:WIN]:
        copy.wait()

    sent = []

    def copy_of(name, src, dst, device):
        n = ids(*name)
        return pltpu.make_async_remote_copy(
            src_ref=src, dst_ref=dst, send_sem=ssem.at[n], recv_sem=rsem.at[n],
            device_id=device, device_id_type=MESH)

    def send(name, src, device, dst=None):
        copy = copy_of(name, src, src if dst is None else dst, device)
        copy.start()
        sent.append(copy)

    def recv(name, dst):
        copy_of(name, dst, dst, at(z, ny, x)).wait_recv()

    right, left = at(z, y, xx(1)), at(z, y, xx(-1))
    other = at(z, ny, x)
    down = {1: at(zz(-1), y, x), -1: at(zz(1), y, x)}
    signs = (1, -1)
    two = pl.ds(0, 2)
    ad, bb = pl.ds(0, 2), pl.ds(2, 2)
    both = pl.ds(0, NY)

    own = g.at[pl.ds(0, WIN), z, y, x]
    send(("x0", 0), g.at[ad, z, y, x], right)
    send(("x0", 1), g.at[ad, z, y, x], left)
    send(("y0", 0), own, other)
    for s in signs:
        send(("z1", s, 0), own, down[s])

    def x_stage(zb):
        def start():
            send(("bx", zb, 0), g.at[bb, zz(zb), both, x], right)
            send(("bx", zb, 1), g.at[bb, zz(zb), both, x], left)

        def forward():
            recv(("bx", zb, 0), g.at[bb, zz(zb), both, xx(-1)])
            send(("bf", zb, 0), g.at[2, zz(zb), both, xx(-1)], right)
            recv(("bx", zb, 1), g.at[bb, zz(zb), both, xx(1)])
            send(("bf", zb, 1), g.at[3, zz(zb), both, xx(1)], left)

        def finish():
            recv(("bf", zb, 0), g.at[2, zz(zb), both, xx(2)])
            recv(("bf", zb, 1), g.at[3, zz(zb), both, xx(2)])

        return start, forward, finish

    def y_start(zb):
        send(("dy", zb), g.at[1, zz(zb), y], other)

    def y_finish(zb):
        recv(("dy", zb), g.at[1, zz(zb), ny])

    stages = {zb: x_stage(zb) for zb in (0, 1, -1, 2, -2, 3, -3, 4)}

    recv(("y0", 0), g.at[pl.ds(0, WIN), z, ny, x])
    for s in signs:
        send(("z1", s, 1), g.at[bb, z, ny, x], down[s])
    recv(("x0", 0), g.at[ad, z, y, xx(-1)])
    send(("xf", 0), g.at[0, z, y, xx(-1)], right)
    recv(("x0", 1), g.at[ad, z, y, xx(1)])
    send(("xf", 1), g.at[1, z, y, xx(1)], left)
    stages[0][0]()
    for n, dx in ((1, -1), (2, 1)):
        send(("y0", n), g.at[ad, z, y, xx(dx)], other)
        for s in signs:
            send(("z1", s, 1 + n), g.at[ad, z, y, xx(dx)], down[s])
    recv(("xf", 0), g.at[0, z, y, xx(2)])
    recv(("xf", 1), g.at[1, z, y, xx(2)])
    send(("y0", 3), g.at[ad, z, y, xx(2)], other)
    for s in signs:
        send(("z1", s, 4), g.at[ad, z, y, xx(2)], down[s])
    for n, dx in ((1, -1), (2, 1), (3, 2)):
        recv(("y0", n), g.at[ad, z, ny, xx(dx)])
    for s in signs:
        send(("z1", s, 5), g.at[0, z, ny], down[s])

    def b_part(k, s):
        zb = zz(s * k)
        if k < 4:
            return g.at[bb, zb, both, x]
        return g.at[2 if s == 1 else 3, zb, both, x]

    def d_part(k, s):
        zb = zz(s * k)
        if k < 4:
            return g.at[1, zb, y]
        return g.at[1, zb, y, pl.ds(0 if s == 1 else 2, 2)]

    def a_part(k, s):
        zb = zz(s * k)
        if k < 4:
            return g.at[0, zb]
        return g.at[0, zb, 0 if s == 1 else 1]

    parts = {"b": b_part, "d": d_part, "a": a_part}

    def pass_on(kind, k, s):
        zb = zz(s * (k - 1))
        if kind == "b":
            src = g.at[bb, zb, both, x] if k < 4 else g.at[2 if s == 1 else 3, zb, both, x]
        elif kind == "d":
            src = g.at[1, zb, y] if k < 4 else g.at[1, zb, y, pl.ds(0 if s == 1 else 2, 2)]
        else:
            src = g.at[0, zb] if k < 4 else g.at[0, zb, 0 if s == 1 else 1]
        send((kind, k, s), src, down[s])

    def take(kind, k, s):
        recv((kind, k, s), parts[kind](k, s))

    def score(w, zb, slot):
        queries = g[w, zb].reshape(2 * LANES, S).astype(EXACT)
        group = lax.dot_general(
            refs8[w], queries, (((1,), (1,)), ((), ())), preferred_element_type=jnp.float32)
        peaks, totals = [], []
        for b in range(NB):
            scores = group[b * BLOCK:(b + 1) * BLOCK]
            peak = jnp.max(scores, axis=0, keepdims=True)
            totals.append(jnp.sum(jnp.exp2((scores - peak) * SCALE_2), axis=0, keepdims=True))
            peaks.append(peak * SCALE)
        shifted = [peaks[b] + pen[b] for b in range(NB)]
        top = functools.reduce(jnp.maximum, shifted)
        total = functools.reduce(
            jnp.add, [totals[b] * jnp.exp(shifted[b] - top) for b in range(NB)])
        part[slot, w] = top + jnp.log(total)

    def blocks_of(k):
        return (0,) if k == 0 else (4,) if k == 4 else (k, -k)

    def compute(k, w_from, w_to):
        n = w_to - w_from
        count = len(blocks_of(k))

        def one(i, carry):
            slot, w = i // n, w_from + i % n
            zb = zz(k * (1 - 2 * slot))
            score(w, zb, slot)
            return carry

        lax.fori_loop(0, n * count, one, 0)

    lane = lax.broadcasted_iota(jnp.int32, (A, LANES), 1) // ROWS

    def plane_send(k):
        count = len(blocks_of(k))
        for slot in range(count):
            for o in range(PLANE):
                half = pl.ds((o // WIN) * LANES, LANES)
                packed = None
                for w in range(WIN):
                    shift = ((w - o) % WIN) * ROWS
                    piece = part[slot, w, :, half]
                    piece = pltpu.roll(piece, shift, 1) if shift else piece
                    packed = piece if packed is None else jnp.where(lane == w, piece, packed)
                sbuf[k, o, slot] = packed
        span = pl.ds(0, count)
        for dy in range(NY):
            for dx in range(NX):
                if dy or dx:
                    ty, tx = (y + dy) % NY, xx(dx)
                    send(("p", k, dy, dx), sbuf.at[k, ty * NX + tx, span], at(z, ty, tx),
                         r1.at[k, dy * NX + dx, span])

    def plane_combine(k):
        count = len(blocks_of(k))
        span = pl.ds(0, count)
        for dy in range(NY):
            for dx in range(NX):
                if dy or dx:
                    recv(("p", k, dy, dx), r1.at[k, dy * NX + dx, span])
        for slot, zb in enumerate(blocks_of(k)):
            mine = lse([sbuf[k, y * NX + x, slot]] + [r1[k, n, slot] for n in range(1, PLANE)])
            n = zb % NZ
            zbuf[n] = mine
            if zb:
                send(("r", n), zbuf.at[n], at(zz(zb), y, x), r2.at[n])

    for s in signs:
        recv(("z1", s, 0), g.at[pl.ds(0, WIN), zz(s), y, x])
        recv(("z1", s, 1), g.at[bb, zz(s), ny, x])
        pass_on("b", 2, s)
        stages[s][0]()
    for s in signs:
        for n, dx in ((2, -1), (3, 1), (4, 2)):
            recv(("z1", s, n), g.at[ad, zz(s), y, xx(dx)])
        pass_on("d", 2, s)
        y_start(s)
    for copy in local[WIN:]:
        copy.wait()
    def narrow(i, carry):
        rows = pl.ds((i % WIN) * (REFS // WIN), REFS // WIN)
        refs8[i // WIN, rows] = refs[i // WIN, rows].astype(EXACT)
        return carry

    lax.fori_loop(0, WIN * WIN, narrow, 0)
    stages[0][1]()
    compute(0, 0, 2)
    for s in signs:
        recv(("z1", s, 5), g.at[0, zz(s), ny])
        pass_on("a", 2, s)
    stages[0][2]()
    compute(0, 2, 4)
    plane_send(0)
    for s in signs:
        stages[s][1]()

    for k in (2, 3):
        for s in signs:
            take("b", k, s)
            pass_on("b", k + 1, s)
            stages[s * k][0]()
        for s in signs:
            take("d", k, s)
            pass_on("d", k + 1, s)
            y_start(s * k)
        for s in signs:
            y_finish(s * (k - 1))
            stages[s * (k - 1)][2]()
        compute(k - 1, 0, 4)
        plane_send(k - 1)
        for s in signs:
            take("a", k, s)
            pass_on("a", k + 1, s)
        for s in signs:
            stages[s * k][1]()
        plane_combine(k - 2)

    for s in signs:
        take("b", 4, s)
    stages[4][0]()
    for s in signs:
        take("d", 4, s)
    y_start(4)
    for s in signs:
        y_finish(s * 3)
        stages[s * 3][2]()
    compute(3, 0, 4)
    plane_send(3)
    stages[4][1]()
    plane_combine(2)
    for s in signs:
        take("a", 4, s)
    y_finish(4)
    compute(4, 0, 2)
    stages[4][2]()
    compute(4, 2, 4)
    plane_send(4)
    plane_combine(3)
    plane_combine(4)

    for n in range(1, NZ):
        recv(("r", n), r2.at[n])
    pooled = lse([zbuf[0]] + [r2[n] for n in range(1, NZ)])
    centered = pooled - jnp.mean(pooled, axis=0, keepdims=True)
    cent[...] = centered
    send(("h", 0), cent, {"win": (win + 1) % WIN}, halo.at[0])
    send(("h", 1), cent, {"win": (win + WIN - 1) % WIN}, halo.at[1])

    def column(read):
        rows = lax.broadcasted_iota(jnp.int32, (A, LANES), 0)
        value = jnp.full((A, LANES), read(0), jnp.float32)
        for a in range(1, A):
            value = jnp.where(rows == a, read(a), value)
        return value

    taps = [column(lambda a, t=t: ker_ref[a, t]) for t in range(TAPS)]
    bias = column(lambda a: bias_ref[a])
    recv(("h", 0), halo.at[0])
    recv(("h", 1), halo.at[1])
    low = jnp.where(win > 0, halo[0], 0.0)
    high = jnp.where(win < WIN - 1, halo[1], 0.0)
    logits = bias
    for t in range(TAPS):
        d = t - TAPS // 2
        if d == 0:
            moved = centered
        elif d < 0:
            shift = (-d * ROWS) % LANES
            moved = low if not shift else jnp.where(
                lane < -d, pltpu.roll(low, shift, 1), pltpu.roll(centered, shift, 1))
        else:
            shift = (-d * ROWS) % LANES
            moved = high if not shift else jnp.where(
                lane >= WIN - d, pltpu.roll(high, shift, 1), pltpu.roll(centered, shift, 1))
        logits = logits + taps[t] * moved
    peak = jnp.max(logits, axis=0, keepdims=True)
    result = logits - peak - jnp.log(jnp.sum(jnp.exp(logits - peak), axis=0, keepdims=True))
    for w in range(WIN):
        out_ref[w] = result[:, w * ROWS:(w + 1) * ROWS]

    for copy in sent:
        copy.wait_send()


MESSAGES = 160


def per_device(queries, references, labels, kernel, class_bias):
    ids = Ids()
    hbm = pl.BlockSpec(memory_space=pl.ANY)
    smem = pl.BlockSpec(memory_space=pltpu.SMEM)
    return pl.pallas_call(
        functools.partial(body, ids),
        out_shape=jax.ShapeDtypeStruct((WIN, A, ROWS), jnp.float32),
        in_specs=[hbm, hbm, smem, smem, smem],
        out_specs=pl.BlockSpec(memory_space=pltpu.VMEM),
        scratch_shapes=[
            pltpu.VMEM((WIN, NZ, NY, NX, ROWS, S), jnp.bfloat16),
            pltpu.VMEM((WIN, REFS, S), jnp.bfloat16),
            pltpu.VMEM((NB, A, 2 * LANES), jnp.float32),
            pltpu.VMEM((2, WIN, A, 2 * LANES), jnp.float32),
            pltpu.VMEM((5, PLANE, 2, A, LANES), jnp.float32),
            pltpu.VMEM((5, PLANE, 2, A, LANES), jnp.float32),
            pltpu.VMEM((NZ, A, LANES), jnp.float32),
            pltpu.VMEM((NZ, A, LANES), jnp.float32),
            pltpu.VMEM((A, LANES), jnp.float32),
            pltpu.VMEM((2, A, LANES), jnp.float32),
            pltpu.VMEM((WIN, REFS, S), EXACT),
            pltpu.SemaphoreType.DMA((MESSAGES,)),
            pltpu.SemaphoreType.DMA((MESSAGES,)),
            pltpu.SemaphoreType.DMA((2 * WIN,)),
        ],
        compiler_params=pltpu.CompilerParams(
            collective_id=0, has_side_effects=True, vmem_limit_bytes=60 * 1024 * 1024),
        cost_estimate=pl.CostEstimate(
            flops=2 * 2048 * REFS * S * WIN, bytes_accessed=5 * 1024 * 1024,
            transcendentals=2048 * REFS * WIN),
    )(queries, references, labels, kernel.T, class_bias)


def solution(mesh):
    in_specs = (P("ref", "win"), P("ref", "win"), P("ref"), P(), P())
    out_specs = P("win", None, "ref")
    return jax.shard_map(
        per_device, mesh=mesh, in_specs=in_specs, out_specs=out_specs, check_vma=False
    )
```
